32 devices in a mesh: grp: 2 (over y), seq: 4 (over x, core), kvh: 4 (over z).
Axes of the slice: x: 2, y: 2, z: 4, core: 2. Of those that a mesh axis runs over, the one named last changes fastest.
Arguments:
- queries: bfloat16 [2048, 8192], P(('grp', 'seq'), 'kvh'), parts along dimension 0, may hold values from -150 to 150
- keys_values: bfloat16 [2, 2048, 1024], P(None, ('grp', 'seq'), 'kvh'), parts along dimension 1, may hold values from -5 to 5
- band_widths: int32 [128], P(('grp', 'kvh')), parts along dimension 0, may hold values from 128 to 2048, as said below
- summary_blocks: int32 [8], P('grp'), parts along dimension 0, may hold values from 0 to 7, as said below
Outputs:
- attended: bfloat16 [2048, 8192], P(('grp', 'seq'), 'kvh'), parts along dimension 0
The draws below stay inside these ranges and needn't reach their ends.
There are 2 independent parts, one for each index of `grp`. The reference program is written for one: setup_inputs(seed, part) draws one part's arguments, and reference() takes and returns one part's arrays. A program takes and returns all parts, laid end to end along the dimension named above; each array names one. Nothing has to cross between parts.
Inputs may be any that keep to these rules, and one draw needn't show every extreme that they name: `band_widths`: some head has a band of exactly 2048 keys in every draw. `summary_blocks`: entry j names a block within positions j * 256 to (j + 1) * 256 - 1.
All inputs are finite; a program needn't handle non-finite values.
Results may differ from the reference program's by a relative error of at most 0.0029.
Values may be sent and summed in bfloat16 or wider, within the bound.
A program may use at most 64 MiB of HBM per device.

```python
import jax
import jax.numpy as jnp
from jax import lax

HEADS = 64
KVH = 8
HD = 128
CTX_DEV = 256
BAND = 2048
SB = 128
CTX = 1024
NSUM = 4


def attention_inputs(key):
    stacked = jnp.clip(jax.random.normal(jax.random.fold_in(key, 101), (2, CTX, KVH * HD), jnp.float32), -5.0, 5.0)
    query_rows = 2.5 * jnp.clip(jax.random.normal(jax.random.fold_in(key, 102), (CTX, HEADS * HD), jnp.float32), -5.0, 5.0)
    return (query_rows, stacked)


def draw_queries(key, part):
    return attention_inputs(key)[0].astype(jnp.bfloat16)


def draw_keys_values(key, part):
    return attention_inputs(key)[1].astype(jnp.bfloat16)


def draw_band_widths(key, part):
    widths = jax.random.randint(jax.random.fold_in(key, 21), (HEADS,), SB, BAND + 1)
    chosen = jax.random.randint(jax.random.fold_in(key, 22), (), 0, HEADS)
    return jnp.where(jnp.arange(HEADS) == chosen, BAND, widths).astype(jnp.int32)


def draw_summary_blocks(key, part):
    per_device = CTX_DEV // SB
    offsets = jax.random.randint(jax.random.fold_in(key, 31), (NSUM,), 0, per_device)
    entries = jnp.arange(NSUM)
    offsets = jnp.where(entries == 0, 0, jnp.where(entries == NSUM - 1, per_device - 1, offsets))
    return (entries * per_device + offsets).astype(jnp.int32)


def setup_inputs(seed: int = 0, part: int = 0) -> dict:
    key_list = jax.random.split(jax.random.key(seed), 5)
    part_splits = jax.random.split(jax.random.fold_in(key_list[4], part), 5)
    queries = draw_queries(jax.random.fold_in(jax.random.fold_in(key_list[4], part), 71), part)
    keys_values = draw_keys_values(jax.random.fold_in(jax.random.fold_in(key_list[4], part), 71), part)
    band_widths = draw_band_widths(jax.random.fold_in(jax.random.fold_in(key_list[4], part), 71), part)
    summary_blocks = draw_summary_blocks(jax.random.fold_in(jax.random.fold_in(key_list[4], part), 71), part)
    return {"queries": queries, "keys_values": keys_values, "band_widths": band_widths, "summary_blocks": summary_blocks}


very_low = -1.0e30


def attend_group(query_group, kv_group, widths, query_pos, band_pos, summary_pos):
    scores = jnp.einsum("crd,kd->rck", query_group.astype(jnp.float32), kv_group[0].astype(jnp.float32)) * (HD ** -0.5)
    limits = query_pos[None, :] - widths[:, None]
    band_vis = (band_pos[None, None, :] > limits[:, :, None]) & (band_pos[None, None, :] <= query_pos[None, :, None]) & (band_pos[None, None, :] >= 0)
    summ_vis = summary_pos[None, None, :] <= limits[:, :, None]
    visible = jnp.concatenate([band_vis, summ_vis], axis=-1)
    best = jnp.max(jnp.where(visible, scores, very_low), axis=-1)
    weights = jnp.where(visible, jnp.exp(scores - best[:, :, None]), 0.0)
    total = jnp.sum(weights, axis=-1)
    rounded = lax.optimization_barrier(weights.astype(jnp.bfloat16))
    mixed = jnp.einsum("rck,kd->crd", rounded.astype(jnp.float32), kv_group[1].astype(jnp.float32))
    return mixed / jnp.transpose(total)[:, :, None]


def reference(queries, keys_values, band_widths, summary_blocks):
    ratio = HEADS // KVH
    padding = jnp.zeros((2, BAND, KVH * HD), keys_values.dtype)
    padded = jnp.concatenate([padding, keys_values], axis=1)
    summary_pos = (summary_blocks[:, None] * SB + jnp.arange(SB, dtype=jnp.int32)[None, :]).reshape(-1).astype(jnp.int32)
    summary_kv = jnp.take(keys_values, summary_pos, axis=1)
    widths = band_widths.reshape(KVH, ratio)

    def one_block(index):
        first = (index * CTX_DEV).astype(jnp.int32)
        window = lax.dynamic_slice_in_dim(padded, first, BAND + CTX_DEV, axis=1)
        band_pos = (first - BAND + jnp.arange(BAND + CTX_DEV, dtype=jnp.int32)).astype(jnp.int32)
        query_pos = (first + jnp.arange(CTX_DEV, dtype=jnp.int32)).astype(jnp.int32)
        all_kv = jnp.concatenate([window, summary_kv], axis=1)
        query_block = lax.dynamic_slice_in_dim(queries, first, CTX_DEV, axis=0).reshape(CTX_DEV, KVH, ratio, HD)
        query_groups = jnp.moveaxis(query_block, 1, 0)
        kv_groups = jnp.moveaxis(all_kv.reshape(2, all_kv.shape[1], KVH, HD), 2, 0)

        def one_group(items):
            query_group, kv_group, width_row = items
            return attend_group(query_group, kv_group, width_row, query_pos, band_pos, summary_pos)

        outputs = lax.map(one_group, (query_groups, kv_groups, widths))
        return jnp.moveaxis(outputs, 0, 1).reshape(CTX_DEV, HEADS * HD).astype(jnp.bfloat16)

    blocks = lax.map(one_block, jnp.arange(CTX // CTX_DEV, dtype=jnp.int32))
    return blocks.reshape(CTX, HEADS * HD)
```

```python
import functools
import math

import jax
import jax.numpy as jnp
from jax import lax
from jax.experimental import pallas as pl
from jax.experimental.pallas import tpu as pltpu
from jax.sharding import PartitionSpec as P

HD = 128
BAND = 2048
SB = 128
ONES = 16
STAT = 8
ALWAYS = 1 << 28
HEAD_UNROLL = 4


very_low = -1e30


def from_behind(block, axis, distance):
    devices = range(lax.axis_size(axis))
    route = [(i - distance, i) for i in devices if i - distance in devices]
    return lax.ppermute(block, axis, route)


def absorb(running, shard_rows, key_pos, summary, grouped, limits, query_pos):
    count = shard_rows.shape[1]
    width = math.gcd(count, 512)
    pieces = count // width
    heads_kv = grouped.shape[1]
    head_dim = grouped.shape[3]
    blocked = jnp.moveaxis(shard_rows.reshape(2, pieces, width, heads_kv, head_dim), 1, 0)
    positions = key_pos.reshape(pieces, width)

    def absorb_block(carried, item):
        block_rows, block_pos = item
        best, total, accum = carried
        scores = jnp.einsum(
            "cgrd,kgd->grck", grouped, block_rows[0], preferred_element_type=jnp.float32
        ) * head_dim ** (-0.5)
        key_line = block_pos[None, None, None, :]
        if summary:
            visible = key_line <= limits[:, :, :, None]
        else:
            visible = (
                (key_line > limits[:, :, :, None])
                & (key_line <= query_pos[None, None, :, None])
                & (key_line >= 0)
            )
        new_best = jnp.maximum(best, jnp.max(jnp.where(visible, scores, very_low), axis=-1))
        weights = jnp.where(visible, jnp.exp(scores - new_best[:, :, :, None]), 0.0)
        fade = jnp.exp(best - new_best)
        total = total * fade + jnp.sum(weights, axis=-1)
        accum = accum * fade[:, :, :, None] + jnp.einsum(
            "grck,kgd->grcd",
            weights.astype(jnp.bfloat16),
            block_rows[1],
            preferred_element_type=jnp.float32,
        )
        return ((new_best, total, accum), None)

    running, unused = lax.scan(absorb_block, running, (blocked, positions))
    return running


def body(queries, keys_values, band_widths, summary_blocks):
    rows = queries.shape[0]
    heads_kv = keys_values.shape[2] // HD
    heads_dev = band_widths.shape[0]
    ratio = heads_dev // heads_kv
    seq_index = lax.axis_index("seq")
    query_pos = seq_index * rows + jnp.arange(rows, dtype=jnp.int32)
    grouped = queries.reshape(rows, heads_kv, ratio, HD)
    limits = query_pos[None, None, :] - band_widths.reshape(heads_kv, ratio)[:, :, None]
    running = (
        jnp.full((heads_kv, ratio, rows), very_low, jnp.float32),
        jnp.zeros((heads_kv, ratio, rows), jnp.float32),
        jnp.zeros((heads_kv, ratio, rows, HD), jnp.float32),
    )
    reach = (BAND - 1) // rows + 1
    local_iota = jnp.arange(rows, dtype=jnp.int32)
    running = absorb(running, keys_values, query_pos, False, grouped, limits, query_pos)
    for distance in range(1, reach + 1):
        earlier = from_behind(keys_values, "seq", distance)
        running = absorb(
            running,
            earlier,
            (seq_index - distance) * rows + local_iota,
            False,
            grouped,
            limits,
            query_pos,
        )
    own_block = lax.dynamic_index_in_dim(summary_blocks, seq_index, 0, keepdims=False)
    local_block = own_block - seq_index * (rows // SB)
    summary_rows = lax.dynamic_slice_in_dim(keys_values, local_block * SB, SB, 1)
    summary_pos = (summary_blocks[:, None] * SB + jnp.arange(SB, dtype=jnp.int32)[None, :]).reshape(
        -1
    )
    gathered = lax.all_gather(summary_rows, "seq", axis=1, tiled=True)
    running = absorb(running, gathered, summary_pos, True, grouped, limits, query_pos)
    best, total, accum = running
    result = accum / total[:, :, :, None]
    return jnp.transpose(result, (2, 0, 1, 3)).reshape(rows, heads_dev * HD).astype(jnp.bfloat16)


def attend_kernel(
    rows, heads_kv, ratio, q_hbm, kv_hbm, widths, blocks, out_hbm,
    q_buf, kv_buf, vt_buf, acc_buf, best_buf, key_buf, out_buf,
    q_sem, own_sem, out_sem, near_send, far_send, pass_send, recv_sem,
):
    me = lax.axis_index("seq")
    core = lax.rem(me, 2)
    partner = me + 1 - 2 * core
    seq_size = lax.axis_size("seq")
    heads = heads_kv * ratio
    scale = math.log2(math.e) * HD ** (-0.5)

    def remote(src, slot, g, send_sem, target):
        return pltpu.make_async_remote_copy(
            src_ref=src,
            dst_ref=kv_buf.at[slot, g],
            send_sem=send_sem,
            recv_sem=recv_sem.at[slot, g],
            device_id={"seq": target},
            device_id_type=pl.DeviceIdType.MESH,
        )

    def own_rows(g):
        return kv_hbm.at[:, :, g * HD : (g + 1) * HD]

    def own_copy(g):
        return pltpu.make_async_copy(own_rows(g), kv_buf.at[me, g], own_sem.at[g])

    def q_copy(h):
        return pltpu.make_async_copy(
            q_hbm.at[:, h * HD : (h + 1) * HD], q_buf.at[h], q_sem.at[h]
        )

    barrier = pltpu.get_barrier_semaphore()
    for step in range(1, seq_size):
        pl.semaphore_signal(
            barrier,
            inc=1,
            device_id={"seq": lax.rem(me + step, seq_size)},
            device_id_type=pl.DeviceIdType.MESH,
        )
    for g in range(heads_kv):
        own_copy(g).start()
    for h in range(heads):
        q_copy(h).start()
    pl.semaphore_wait(barrier, seq_size - 1)

    for g in range(heads_kv):

        @pl.when(me < 2)
        def _():
            remote(own_rows(g), me, g, far_send.at[g], me + 2).start()

        @pl.when(core == 0)
        def _():
            remote(own_rows(g), me, g, near_send.at[g], me + 1).start()

    for slot in range(seq_size):
        pos = slot * rows + lax.broadcasted_iota(jnp.int32, (rows, HD), 0)
        first = blocks[slot] * SB
        in_summary = (pos >= first) & (pos < first + SB)
        key_buf[slot] = jnp.where(in_summary, ALWAYS, pos)
    for g in range(heads_kv):
        vt_buf[g, HD:, :] = jnp.ones((ONES, rows), jnp.bfloat16)

    row_pos = me * rows + lax.broadcasted_iota(jnp.int32, (1, rows), 1)

    def heads_of(slot, g, is_own):
        vt_buf[g, :HD, :] = kv_buf[slot, g, 1].astype(jnp.float32).T.astype(jnp.bfloat16)

        def one_head(r, unused):
            h = g * ratio + r
            scores = lax.dot_general(
                kv_buf[slot, g, 0],
                q_buf[h],
                (((1,), (1,)), ((), ())),
                preferred_element_type=jnp.float32,
            )
            limit = row_pos - widths[h]
            lanes = key_buf[slot]
            keys = jnp.concatenate([lanes] * (rows // HD), axis=1)
            visible = keys > limit
            if is_own:
                visible = visible & (
                    lax.broadcasted_iota(jnp.int32, (rows, rows), 0)
                    <= lax.broadcasted_iota(jnp.int32, (rows, rows), 1)
                )
            scores = jnp.where(visible, scores, -1e30)
            top = jnp.max(scores, axis=0, keepdims=True)
            if not is_own:
                old = best_buf[h]
                top = jnp.maximum(old, top)
            weights = jnp.exp2((scores - top) * scale).astype(jnp.bfloat16)
            part = lax.dot_general(
                vt_buf[g],
                weights,
                (((1,), (0,)), ((), ())),
                preferred_element_type=jnp.float32,
            )[: HD + STAT]
            if not is_own:
                part = part + acc_buf[h] * jnp.exp2((old - top) * scale)
            acc_buf[h] = part
            best_buf[h] = top
            return unused

        lax.fori_loop(0, ratio, one_head, 0, unroll=HEAD_UNROLL)

    for g in range(heads_kv):
        own_copy(g).wait()
    for h in range(heads):
        q_copy(h).wait()

    def own_step(g, unused):
        heads_of(me, g, True)
        return unused

    lax.fori_loop(0, heads_kv, own_step, 0)

    near = heads_kv * core

    def other_step(item, unused):
        far = item - near
        is_near = item < near
        far_slot = jnp.where(lax.rem(far, 2) == 0, core, 1 - core)
        slot = jnp.where(is_near, me - 1, far_slot)
        g = jnp.where(is_near, item, far // 2)
        remote(kv_buf.at[slot, g], slot, g, pass_send.at[g], partner).wait_recv()

        @pl.when((me >= 2) & (slot == core))
        def _():
            remote(kv_buf.at[slot, g], slot, g, pass_send.at[g], partner).start()

        heads_of(slot, g, False)
        return unused

    lax.fori_loop(0, heads_kv * me, other_step, 0)

    def out_copy(h):
        return pltpu.make_async_copy(
            out_buf.at[h],
            out_hbm.at[:, pl.ds(pl.multiple_of(h * HD, HD), HD)],
            out_sem.at[h],
        )

    def finish(h, unused):
        total = acc_buf[h, HD : HD + 1, :]
        result = acc_buf[h, :HD, :] * (1.0 / total)
        out_buf[h] = result.T.astype(jnp.bfloat16)
        out_copy(h).start()
        return unused

    lax.fori_loop(0, heads, finish, 0, unroll=4)

    for g in range(heads_kv):

        @pl.when(me < 2)
        def _():
            remote(own_rows(g), me, g, far_send.at[g], me + 2).wait_send()

        @pl.when(core == 0)
        def _():
            remote(own_rows(g), me, g, near_send.at[g], me + 1).wait_send()

        @pl.when(me >= 2)
        def _():
            remote(kv_buf.at[core, g], core, g, pass_send.at[g], partner).wait_send()

    for h in range(heads):
        out_copy(h).wait()


def fused_body(queries, keys_values, band_widths, summary_blocks):
    rows = queries.shape[0]
    heads_kv = keys_values.shape[2] // HD
    heads = band_widths.shape[0]
    seq_size = lax.axis_size("seq")
    anywhere = pl.BlockSpec(memory_space=pl.ANY)
    scalars = pl.BlockSpec(memory_space=pltpu.SMEM)
    dma = pltpu.SemaphoreType.DMA
    return pl.pallas_call(
        functools.partial(attend_kernel, rows, heads_kv, heads // heads_kv),
        out_shape=jax.ShapeDtypeStruct(queries.shape, jnp.bfloat16),
        in_specs=[anywhere, anywhere, scalars, scalars],
        out_specs=anywhere,
        scratch_shapes=[
            pltpu.VMEM((heads, rows, HD), jnp.bfloat16),
            pltpu.VMEM((seq_size, heads_kv, 2, rows, HD), jnp.bfloat16),
            pltpu.VMEM((heads_kv, HD + ONES, rows), jnp.bfloat16),
            pltpu.VMEM((heads, HD + STAT, rows), jnp.float32),
            pltpu.VMEM((heads, 1, rows), jnp.float32),
            pltpu.VMEM((seq_size, rows, HD), jnp.int32),
            pltpu.VMEM((heads, rows, HD), jnp.bfloat16),
            dma((heads,)),
            dma((heads_kv,)),
            dma((heads,)),
            dma((heads_kv,)),
            dma((heads_kv,)),
            dma((heads_kv,)),
            dma((seq_size, heads_kv)),
        ],
        compiler_params=pltpu.CompilerParams(
            collective_id=0,
            has_side_effects=True,
            vmem_limit_bytes=32 * 1024 * 1024,
        ),
        cost_estimate=pl.CostEstimate(
            flops=4 * heads * rows * rows * seq_size * HD,
            bytes_accessed=4 * queries.size,
            transcendentals=heads * rows * rows * seq_size,
        ),
    )(queries, keys_values, band_widths, summary_blocks)


def dispatch(queries, keys_values, band_widths, summary_blocks):
    rows = queries.shape[0]
    seq_size = lax.axis_size("seq")
    two_chips = seq_size == 4 and summary_blocks.shape[0] == seq_size
    if two_chips and seq_size * rows <= BAND and rows % (2 * SB) == 0:
        return fused_body(queries, keys_values, band_widths, summary_blocks)
    return body(queries, keys_values, band_widths, summary_blocks)


def solution(mesh):
    return jax.shard_map(
        dispatch,
        mesh=mesh,
        in_specs=(
            P(("grp", "seq"), "kvh"),
            P(None, ("grp", "seq"), "kvh"),
            P(("grp", "kvh")),
            P("grp"),
        ),
        out_specs=P(("grp", "seq"), "kvh"),
        check_vma=False,
    )
```

```python
import functools
import math

import jax
import jax.numpy as jnp
from jax import lax
from jax.experimental import pallas as pl
from jax.experimental.pallas import tpu as pltpu
from jax.sharding import PartitionSpec as P

HD = 128
BAND = 2048
SB = 128
ONES = 16
STAT = 8
ALWAYS = 1 << 28


very_low = -1e30


def from_behind(block, axis, distance):
    devices = range(lax.axis_size(axis))
    route = [(i - distance, i) for i in devices if i - distance in devices]
    return lax.ppermute(block, axis, route)


def absorb(running, shard_rows, key_pos, summary, grouped, limits, query_pos):
    count = shard_rows.shape[1]
    width = math.gcd(count, 512)
    pieces = count // width
    heads_kv = grouped.shape[1]
    head_dim = grouped.shape[3]
    blocked = jnp.moveaxis(shard_rows.reshape(2, pieces, width, heads_kv, head_dim), 1, 0)
    positions = key_pos.reshape(pieces, width)

    def absorb_block(carried, item):
        block_rows, block_pos = item
        best, total, accum = carried
        scores = jnp.einsum(
            "cgrd,kgd->grck", grouped, block_rows[0], preferred_element_type=jnp.float32
        ) * head_dim ** (-0.5)
        key_line = block_pos[None, None, None, :]
        if summary:
            visible = key_line <= limits[:, :, :, None]
        else:
            visible = (
                (key_line > limits[:, :, :, None])
                & (key_line <= query_pos[None, None, :, None])
                & (key_line >= 0)
            )
        new_best = jnp.maximum(best, jnp.max(jnp.where(visible, scores, very_low), axis=-1))
        weights = jnp.where(visible, jnp.exp(scores - new_best[:, :, :, None]), 0.0)
        fade = jnp.exp(best - new_best)
        total = total * fade + jnp.sum(weights, axis=-1)
        accum = accum * fade[:, :, :, None] + jnp.einsum(
            "grck,kgd->grcd",
            weights.astype(jnp.bfloat16),
            block_rows[1],
            preferred_element_type=jnp.float32,
        )
        return ((new_best, total, accum), None)

    running, unused = lax.scan(absorb_block, running, (blocked, positions))
    return running


def body(queries, keys_values, band_widths, summary_blocks):
    rows = queries.shape[0]
    heads_kv = keys_values.shape[2] // HD
    heads_dev = band_widths.shape[0]
    ratio = heads_dev // heads_kv
    seq_index = lax.axis_index("seq")
    query_pos = seq_index * rows + jnp.arange(rows, dtype=jnp.int32)
    grouped = queries.reshape(rows, heads_kv, ratio, HD)
    limits = query_pos[None, None, :] - band_widths.reshape(heads_kv, ratio)[:, :, None]
    running = (
        jnp.full((heads_kv, ratio, rows), very_low, jnp.float32),
        jnp.zeros((heads_kv, ratio, rows), jnp.float32),
        jnp.zeros((heads_kv, ratio, rows, HD), jnp.float32),
    )
    reach = (BAND - 1) // rows + 1
    local_iota = jnp.arange(rows, dtype=jnp.int32)
    running = absorb(running, keys_values, query_pos, False, grouped, limits, query_pos)
    for distance in range(1, reach + 1):
        earlier = from_behind(keys_values, "seq", distance)
        running = absorb(
            running,
            earlier,
            (seq_index - distance) * rows + local_iota,
            False,
            grouped,
            limits,
            query_pos,
        )
    own_block = lax.dynamic_index_in_dim(summary_blocks, seq_index, 0, keepdims=False)
    local_block = own_block - seq_index * (rows // SB)
    summary_rows = lax.dynamic_slice_in_dim(keys_values, local_block * SB, SB, 1)
    summary_pos = (summary_blocks[:, None] * SB + jnp.arange(SB, dtype=jnp.int32)[None, :]).reshape(
        -1
    )
    gathered = lax.all_gather(summary_rows, "seq", axis=1, tiled=True)
    running = absorb(running, gathered, summary_pos, True, grouped, limits, query_pos)
    best, total, accum = running
    result = accum / total[:, :, :, None]
    return jnp.transpose(result, (2, 0, 1, 3)).reshape(rows, heads_dev * HD).astype(jnp.bfloat16)


def attend_kernel(
    rows, heads_kv, ratio, q_hbm, kv_hbm, widths, blocks, out_hbm,
    q_buf, kv_buf, vt_buf, acc_buf, best_buf, key_buf, own_keys, out_buf,
    q_sem, own_sem, out_sem, near_send, far_send, pass_send, recv_sem,
):
    me = lax.axis_index("seq")
    core = lax.rem(me, 2)
    partner = me + 1 - 2 * core
    seq_size = lax.axis_size("seq")
    heads = heads_kv * ratio
    scale = math.log2(math.e) * HD ** (-0.5)

    def remote(src, slot, g, send_sem, target):
        return pltpu.make_async_remote_copy(
            src_ref=src,
            dst_ref=kv_buf.at[slot, g],
            send_sem=send_sem,
            recv_sem=recv_sem.at[slot, g],
            device_id={"seq": target},
            device_id_type=pl.DeviceIdType.MESH,
        )

    def own_rows(g):
        return kv_hbm.at[:, :, g * HD : (g + 1) * HD]

    def own_copy(g):
        return pltpu.make_async_copy(own_rows(g), kv_buf.at[me, g], own_sem.at[g])

    def q_copy(h):
        return pltpu.make_async_copy(
            q_hbm.at[:, h * HD : (h + 1) * HD],
            q_buf.at[h // ratio, h % ratio],
            q_sem.at[h],
        )

    barrier = pltpu.get_barrier_semaphore()
    for step in range(1, seq_size):
        pl.semaphore_signal(
            barrier,
            inc=1,
            device_id={"seq": lax.rem(me + step, seq_size)},
            device_id_type=pl.DeviceIdType.MESH,
        )
    for g in range(heads_kv):
        own_copy(g).start()
    for h in range(heads):
        q_copy(h).start()
    pl.semaphore_wait(barrier, seq_size - 1)

    for g in range(heads_kv):

        @pl.when(me < 2)
        def _():
            remote(own_rows(g), me, g, far_send.at[g], me + 2).start()

        @pl.when(core == 0)
        def _():
            remote(own_rows(g), me, g, near_send.at[g], me + 1).start()

    for slot in range(seq_size):
        pos = slot * rows + lax.broadcasted_iota(jnp.int32, (rows, HD), 0)
        first = blocks[slot] * SB
        in_summary = (pos >= first) & (pos < first + SB)
        key_buf[slot] = jnp.where(in_summary, ALWAYS, pos)
    own_cols = lax.broadcasted_iota(jnp.int32, (rows, rows), 1)
    own_down = lax.broadcasted_iota(jnp.int32, (rows, rows), 0)
    own_line = jnp.concatenate([key_buf[me]] * (rows // HD), axis=1)
    own_keys[...] = jnp.where(own_down <= own_cols, own_line, -ALWAYS)
    for g in range(heads_kv):
        vt_buf[g, HD:, :] = jnp.ones((ONES, rows), jnp.bfloat16)

    row_pos = me * rows + lax.broadcasted_iota(jnp.int32, (1, rows), 1)

    def heads_of(slot, g, is_own):
        vt_buf[g, :HD, :] = kv_buf[slot, g, 1].astype(jnp.float32).T.astype(jnp.bfloat16)

        def score(r):
            return lax.dot_general(
                kv_buf[slot, g, 0],
                q_buf[g, r],
                (((1,), (1,)), ((), ())),
                preferred_element_type=jnp.float32,
            )

        def soften(r, scores):
            limit = row_pos - widths[g * ratio + r]
            if is_own:
                keys = own_keys[...]
            else:
                keys = jnp.concatenate([key_buf[slot]] * (rows // HD), axis=1)
            scores = jnp.where(keys > limit, scores, -1e30)
            top = jnp.max(scores, axis=0, keepdims=True)
            fade = None
            if not is_own:
                old = best_buf[g, r]
                top = jnp.maximum(old, top)
                fade = jnp.exp2((old - top) * scale)
            best_buf[g, r] = top
            return jnp.exp2((scores - top) * scale).astype(jnp.bfloat16), fade

        def mix(r, weights, fade):
            part = lax.dot_general(
                vt_buf[g],
                weights,
                (((1,), (0,)), ((), ())),
                preferred_element_type=jnp.float32,
            )[: HD + STAT]
            if fade is not None:
                part = part + acc_buf[g, r] * fade
            acc_buf[g, r] = part

        scores = score(0)
        waiting = None
        for r in range(ratio):
            following = score(r + 1) if r + 1 < ratio else None
            if waiting is not None:
                mix(*waiting)
            waiting = (r, *soften(r, scores))
            scores = following
        mix(*waiting)

    for g in range(heads_kv):
        own_copy(g).wait()
    for h in range(heads):
        q_copy(h).wait()

    def own_step(g, unused):
        heads_of(me, g, True)
        return unused

    lax.fori_loop(0, heads_kv, own_step, 0)

    near = heads_kv * core

    def other_step(item, unused):
        far = item - near
        is_near = item < near
        far_slot = jnp.where(lax.rem(far, 2) == 0, core, 1 - core)
        slot = jnp.where(is_near, me - 1, far_slot)
        g = jnp.where(is_near, item, far // 2)
        remote(kv_buf.at[slot, g], slot, g, pass_send.at[g], partner).wait_recv()

        @pl.when((me >= 2) & (slot == core))
        def _():
            remote(kv_buf.at[slot, g], slot, g, pass_send.at[g], partner).start()

        heads_of(slot, g, False)
        return unused

    lax.fori_loop(0, heads_kv * me, other_step, 0)

    def out_copy(h):
        return pltpu.make_async_copy(
            out_buf.at[h],
            out_hbm.at[:, pl.ds(pl.multiple_of(h * HD, HD), HD)],
            out_sem.at[h],
        )

    def finish(h, unused):
        g, r = h // ratio, h % ratio
        total = acc_buf[g, r, HD : HD + 1, :]
        result = acc_buf[g, r, :HD, :] * (1.0 / total)
        out_buf[h] = result.T.astype(jnp.bfloat16)
        out_copy(h).start()
        return unused

    lax.fori_loop(0, heads, finish, 0, unroll=4)

    for g in range(heads_kv):

        @pl.when(me < 2)
        def _():
            remote(own_rows(g), me, g, far_send.at[g], me + 2).wait_send()

        @pl.when(core == 0)
        def _():
            remote(own_rows(g), me, g, near_send.at[g], me + 1).wait_send()

        @pl.when(me >= 2)
        def _():
            remote(kv_buf.at[core, g], core, g, pass_send.at[g], partner).wait_send()

    for h in range(heads):
        out_copy(h).wait()


def fused_body(queries, keys_values, band_widths, summary_blocks):
    rows = queries.shape[0]
    heads_kv = keys_values.shape[2] // HD
    heads = band_widths.shape[0]
    ratio = heads // heads_kv
    seq_size = lax.axis_size("seq")
    outside = pl.BlockSpec(memory_space=pltpu.HBM)
    scalars = pl.BlockSpec(memory_space=pltpu.SMEM)
    dma = pltpu.SemaphoreType.DMA
    return pl.pallas_call(
        functools.partial(attend_kernel, rows, heads_kv, ratio),
        out_shape=jax.ShapeDtypeStruct(queries.shape, jnp.bfloat16),
        in_specs=[outside, outside, scalars, scalars],
        out_specs=outside,
        scratch_shapes=[
            pltpu.VMEM((heads_kv, ratio, rows, HD), jnp.bfloat16),
            pltpu.VMEM((seq_size, heads_kv, 2, rows, HD), jnp.bfloat16),
            pltpu.VMEM((heads_kv, HD + ONES, rows), jnp.bfloat16),
            pltpu.VMEM((heads_kv, ratio, HD + STAT, rows), jnp.float32),
            pltpu.VMEM((heads_kv, ratio, 1, rows), jnp.float32),
            pltpu.VMEM((seq_size, rows, HD), jnp.int32),
            pltpu.VMEM((rows, rows), jnp.int32),
            pltpu.VMEM((heads, rows, HD), jnp.bfloat16),
            dma((heads,)),
            dma((heads_kv,)),
            dma((heads,)),
            dma((heads_kv,)),
            dma((heads_kv,)),
            dma((heads_kv,)),
            dma((seq_size, heads_kv)),
        ],
        compiler_params=pltpu.CompilerParams(
            collective_id=0,
            has_side_effects=True,
            vmem_limit_bytes=32 * 1024 * 1024,
        ),
        cost_estimate=pl.CostEstimate(
            flops=4 * heads * rows * rows * seq_size * HD,
            bytes_accessed=4 * queries.size,
            transcendentals=heads * rows * rows * seq_size,
        ),
    )(queries, keys_values, band_widths, summary_blocks)


def dispatch(queries, keys_values, band_widths, summary_blocks):
    rows = queries.shape[0]
    seq_size = lax.axis_size("seq")
    two_chips = seq_size == 4 and summary_blocks.shape[0] == seq_size
    if two_chips and seq_size * rows <= BAND and rows % (2 * SB) == 0:
        return fused_body(queries, keys_values, band_widths, summary_blocks)
    return body(queries, keys_values, band_widths, summary_blocks)


def solution(mesh):
    return jax.shard_map(
        dispatch,
        mesh=mesh,
        in_specs=(
            P(("grp", "seq"), "kvh"),
            P(None, ("grp", "seq"), "kvh"),
            P(("grp", "kvh")),
            P("grp"),
        ),
        out_specs=P(("grp", "seq"), "kvh"),
        check_vma=False,
    )
```

```python
import functools
import math

import jax
import jax.numpy as jnp
from jax import lax
from jax.experimental import pallas as pl
from jax.experimental.pallas import tpu as pltpu
from jax.sharding import PartitionSpec as P

HD = 128
BAND = 2048
SB = 128
ONES = 16
STAT = 8
ALWAYS = 1 << 28


very_low = -1e30


def from_behind(block, axis, distance):
    devices = range(lax.axis_size(axis))
    route = [(i - distance, i) for i in devices if i - distance in devices]
    return lax.ppermute(block, axis, route)


def absorb(running, shard_rows, key_pos, summary, grouped, limits, query_pos):
    count = shard_rows.shape[1]
    width = math.gcd(count, 512)
    pieces = count // width
    heads_kv = grouped.shape[1]
    head_dim = grouped.shape[3]
    blocked = jnp.moveaxis(shard_rows.reshape(2, pieces, width, heads_kv, head_dim), 1, 0)
    positions = key_pos.reshape(pieces, width)

    def absorb_block(carried, item):
        block_rows, block_pos = item
        best, total, accum = carried
        scores = jnp.einsum(
            "cgrd,kgd->grck", grouped, block_rows[0], preferred_element_type=jnp.float32
        ) * head_dim ** (-0.5)
        key_line = block_pos[None, None, None, :]
        if summary:
            visible = key_line <= limits[:, :, :, None]
        else:
            visible = (
                (key_line > limits[:, :, :, None])
                & (key_line <= query_pos[None, None, :, None])
                & (key_line >= 0)
            )
        new_best = jnp.maximum(best, jnp.max(jnp.where(visible, scores, very_low), axis=-1))
        weights = jnp.where(visible, jnp.exp(scores - new_best[:, :, :, None]), 0.0)
        fade = jnp.exp(best - new_best)
        total = total * fade + jnp.sum(weights, axis=-1)
        accum = accum * fade[:, :, :, None] + jnp.einsum(
            "grck,kgd->grcd",
            weights.astype(jnp.bfloat16),
            block_rows[1],
            preferred_element_type=jnp.float32,
        )
        return ((new_best, total, accum), None)

    running, unused = lax.scan(absorb_block, running, (blocked, positions))
    return running


def body(queries, keys_values, band_widths, summary_blocks):
    rows = queries.shape[0]
    heads_kv = keys_values.shape[2] // HD
    heads_dev = band_widths.shape[0]
    ratio = heads_dev // heads_kv
    seq_index = lax.axis_index("seq")
    query_pos = seq_index * rows + jnp.arange(rows, dtype=jnp.int32)
    grouped = queries.reshape(rows, heads_kv, ratio, HD)
    limits = query_pos[None, None, :] - band_widths.reshape(heads_kv, ratio)[:, :, None]
    running = (
        jnp.full((heads_kv, ratio, rows), very_low, jnp.float32),
        jnp.zeros((heads_kv, ratio, rows), jnp.float32),
        jnp.zeros((heads_kv, ratio, rows, HD), jnp.float32),
    )
    reach = (BAND - 1) // rows + 1
    local_iota = jnp.arange(rows, dtype=jnp.int32)
    running = absorb(running, keys_values, query_pos, False, grouped, limits, query_pos)
    for distance in range(1, reach + 1):
        earlier = from_behind(keys_values, "seq", distance)
        running = absorb(
            running,
            earlier,
            (seq_index - distance) * rows + local_iota,
            False,
            grouped,
            limits,
            query_pos,
        )
    own_block = lax.dynamic_index_in_dim(summary_blocks, seq_index, 0, keepdims=False)
    local_block = own_block - seq_index * (rows // SB)
    summary_rows = lax.dynamic_slice_in_dim(keys_values, local_block * SB, SB, 1)
    summary_pos = (summary_blocks[:, None] * SB + jnp.arange(SB, dtype=jnp.int32)[None, :]).reshape(
        -1
    )
    gathered = lax.all_gather(summary_rows, "seq", axis=1, tiled=True)
    running = absorb(running, gathered, summary_pos, True, grouped, limits, query_pos)
    best, total, accum = running
    result = accum / total[:, :, :, None]
    return jnp.transpose(result, (2, 0, 1, 3)).reshape(rows, heads_dev * HD).astype(jnp.bfloat16)


def attend_kernel(
    rows, heads_kv, ratio, q_hbm, kv_hbm, widths, blocks, out_hbm,
    q_buf, kv_buf, vt_buf, acc_buf, best_buf, key_buf, own_keys, out_buf,
    q_sem, own_sem, out_sem, near_send, far_send, pass_send, recv_sem,
):
    me = lax.axis_index("seq")
    core = lax.rem(me, 2)
    partner = me + 1 - 2 * core
    seq_size = lax.axis_size("seq")
    heads = heads_kv * ratio
    scale = math.log2(math.e) * HD ** (-0.5)

    def remote(src, slot, g, send_sem, target):
        return pltpu.make_async_remote_copy(
            src_ref=src,
            dst_ref=kv_buf.at[slot, g],
            send_sem=send_sem,
            recv_sem=recv_sem.at[slot, g],
            device_id={"seq": target},
            device_id_type=pl.DeviceIdType.MESH,
        )

    def own_rows(g):
        return kv_hbm.at[:, :, g * HD : (g + 1) * HD]

    def own_copy(g):
        return pltpu.make_async_copy(own_rows(g), kv_buf.at[me, g], own_sem.at[g])

    def q_copy(h):
        return pltpu.make_async_copy(
            q_hbm.at[:, h * HD : (h + 1) * HD],
            q_buf.at[h // ratio, h % ratio],
            q_sem.at[h],
        )

    barrier = pltpu.get_barrier_semaphore()
    for step in range(1, seq_size):
        pl.semaphore_signal(
            barrier,
            inc=1,
            device_id={"seq": lax.rem(me + step, seq_size)},
            device_id_type=pl.DeviceIdType.MESH,
        )
    for g in range(heads_kv):
        own_copy(g).start()
    for h in range(heads):
        q_copy(h).start()
    pl.semaphore_wait(barrier, seq_size - 1)

    for g in range(heads_kv):
        own_copy(g).wait()

        @pl.when(me < 2)
        def _():
            remote(kv_buf.at[me, g], me, g, far_send.at[g], me + 2).start()

        @pl.when(core == 0)
        def _():
            remote(kv_buf.at[me, g], me, g, near_send.at[g], me + 1).start()

    for slot in range(seq_size):
        pos = slot * rows + lax.broadcasted_iota(jnp.int32, (rows, HD), 0)
        first = blocks[slot] * SB
        in_summary = (pos >= first) & (pos < first + SB)
        key_buf[slot] = jnp.where(in_summary, ALWAYS, pos)
    own_cols = lax.broadcasted_iota(jnp.int32, (rows, rows), 1)
    own_down = lax.broadcasted_iota(jnp.int32, (rows, rows), 0)
    own_line = jnp.concatenate([key_buf[me]] * (rows // HD), axis=1)
    own_keys[...] = jnp.where(own_down <= own_cols, own_line, -ALWAYS)
    for g in range(heads_kv):
        vt_buf[g, HD:, :] = jnp.ones((ONES, rows), jnp.bfloat16)

    row_pos = me * rows + lax.broadcasted_iota(jnp.int32, (1, rows), 1)

    def heads_of(slot, g, is_own):
        vt_buf[g, :HD, :] = kv_buf[slot, g, 1].astype(jnp.float32).T.astype(jnp.bfloat16)

        def score(r):
            return lax.dot_general(
                kv_buf[slot, g, 0],
                q_buf[g, r],
                (((1,), (1,)), ((), ())),
                preferred_element_type=jnp.float32,
            )

        def soften(r, scores):
            limit = row_pos - widths[g * ratio + r]
            if is_own:
                keys = own_keys[...]
            else:
                keys = jnp.concatenate([key_buf[slot]] * (rows // HD), axis=1)
            scores = jnp.where(keys > limit, scores, -1e30)
            top = jnp.max(scores, axis=0, keepdims=True)
            fade = None
            if not is_own:
                old = best_buf[g, r]
                top = jnp.maximum(old, top)
                fade = jnp.exp2((old - top) * scale)
            best_buf[g, r] = top
            return jnp.exp2((scores - top) * scale).astype(jnp.bfloat16), fade

        def mix(r, weights, fade):
            part = lax.dot_general(
                vt_buf[g],
                weights,
                (((1,), (0,)), ((), ())),
                preferred_element_type=jnp.float32,
            )[: HD + STAT]
            if fade is not None:
                part = part + acc_buf[g, r] * fade
            acc_buf[g, r] = part

        scores = score(0)
        waiting = None
        for r in range(ratio):
            following = score(r + 1) if r + 1 < ratio else None
            if waiting is not None:
                mix(*waiting)
            waiting = (r, *soften(r, scores))
            scores = following
        mix(*waiting)

    for h in range(heads):
        q_copy(h).wait()

    def own_step(g, unused):
        heads_of(me, g, True)
        return unused

    lax.fori_loop(0, heads_kv, own_step, 0)

    def out_copy(h):
        return pltpu.make_async_copy(
            out_buf.at[h],
            out_hbm.at[:, pl.ds(pl.multiple_of(h * HD, HD), HD)],
            out_sem.at[h],
        )

    def finish(g):
        for r in range(ratio):
            total = acc_buf[g, r, HD : HD + 1, :]
            result = acc_buf[g, r, :HD, :] * (1.0 / total)
            out_buf[g * ratio + r] = result.T.astype(out_buf.dtype)
        for r in range(ratio):
            out_copy(g * ratio + r).start()

    near = heads_kv * core

    def other_step(item, unused):
        far = item - near
        is_near = item < near
        far_slot = jnp.where(lax.rem(far, 2) == 0, core, 1 - core)
        slot = jnp.where(is_near, me - 1, far_slot)
        g = jnp.where(is_near, item, far // 2)
        remote(kv_buf.at[slot, g], slot, g, pass_send.at[g], partner).wait_recv()

        @pl.when((me >= 2) & (slot == core))
        def _():
            remote(kv_buf.at[slot, g], slot, g, pass_send.at[g], partner).start()

        heads_of(slot, g, False)

        @pl.when((me >= 2) & (item >= near) & (lax.rem(far, 2) == 1))
        def _():
            finish(g)

        return unused

    lax.fori_loop(0, heads_kv * me, other_step, 0)

    def last_step(g, unused):
        finish(g)
        return unused

    lax.fori_loop(0, jnp.where(me < 2, heads_kv, 0), last_step, 0)

    for g in range(heads_kv):

        @pl.when(me < 2)
        def _():
            remote(kv_buf.at[me, g], me, g, far_send.at[g], me + 2).wait_send()

        @pl.when(core == 0)
        def _():
            remote(kv_buf.at[me, g], me, g, near_send.at[g], me + 1).wait_send()

        @pl.when(me >= 2)
        def _():
            remote(kv_buf.at[core, g], core, g, pass_send.at[g], partner).wait_send()

    for h in range(heads):
        out_copy(h).wait()


def fused_body(queries, keys_values, band_widths, summary_blocks):
    rows = queries.shape[0]
    heads_kv = keys_values.shape[2] // HD
    heads = band_widths.shape[0]
    ratio = heads // heads_kv
    seq_size = lax.axis_size("seq")
    outside = pl.BlockSpec(memory_space=pltpu.HBM)
    scalars = pl.BlockSpec(memory_space=pltpu.SMEM)
    dma = pltpu.SemaphoreType.DMA
    return pl.pallas_call(
        functools.partial(attend_kernel, rows, heads_kv, ratio),
        out_shape=jax.ShapeDtypeStruct(queries.shape, jnp.bfloat16),
        in_specs=[outside, outside, scalars, scalars],
        out_specs=outside,
        scratch_shapes=[
            pltpu.VMEM((heads_kv, ratio, rows, HD), jnp.bfloat16),
            pltpu.VMEM((seq_size, heads_kv, 2, rows, HD), jnp.bfloat16),
            pltpu.VMEM((heads_kv, HD + ONES, rows), jnp.bfloat16),
            pltpu.VMEM((heads_kv, ratio, HD + STAT, rows), jnp.float32),
            pltpu.VMEM((heads_kv, ratio, 1, rows), jnp.float32),
            pltpu.VMEM((seq_size, rows, HD), jnp.int32),
            pltpu.VMEM((rows, rows), jnp.int32),
            pltpu.VMEM((heads, rows, HD), jnp.bfloat16),
            dma((heads,)),
            dma((heads_kv,)),
            dma((heads,)),
            dma((heads_kv,)),
            dma((heads_kv,)),
            dma((heads_kv,)),
            dma((seq_size, heads_kv)),
        ],
        compiler_params=pltpu.CompilerParams(
            collective_id=0,
            has_side_effects=True,
            vmem_limit_bytes=63 * 1024 * 1024,
        ),
        cost_estimate=pl.CostEstimate(
            flops=4 * heads * rows * rows * seq_size * HD,
            bytes_accessed=4 * queries.size,
            transcendentals=heads * rows * rows * seq_size,
        ),
    )(queries, keys_values, band_widths, summary_blocks)


def dispatch(queries, keys_values, band_widths, summary_blocks):
    rows = queries.shape[0]
    seq_size = lax.axis_size("seq")
    two_chips = seq_size == 4 and summary_blocks.shape[0] == seq_size
    if two_chips and seq_size * rows <= BAND and rows % (2 * SB) == 0:
        return fused_body(queries, keys_values, band_widths, summary_blocks)
    return body(queries, keys_values, band_widths, summary_blocks)


def solution(mesh):
    return jax.shard_map(
        dispatch,
        mesh=mesh,
        in_specs=(
            P(("grp", "seq"), "kvh"),
            P(None, ("grp", "seq"), "kvh"),
            P(("grp", "kvh")),
            P("grp"),
        ),
        out_specs=P(("grp", "seq"), "kvh"),
        check_vma=False,
    )
```

```python
import functools
import math

import jax
import jax.numpy as jnp
from jax import lax
from jax.experimental import pallas as pl
from jax.experimental.pallas import tpu as pltpu
from jax.sharding import PartitionSpec as P

HD = 128
BAND = 2048
SB = 128
ONES = 16
STAT = 8
ALWAYS = 1 << 28


very_low = -1e30


def from_behind(block, axis, distance):
    devices = range(lax.axis_size(axis))
    route = [(i - distance, i) for i in devices if i - distance in devices]
    return lax.ppermute(block, axis, route)


def absorb(running, shard_rows, key_pos, summary, grouped, limits, query_pos):
    count = shard_rows.shape[1]
    width = math.gcd(count, 512)
    pieces = count // width
    heads_kv = grouped.shape[1]
    head_dim = grouped.shape[3]
    blocked = jnp.moveaxis(shard_rows.reshape(2, pieces, width, heads_kv, head_dim), 1, 0)
    positions = key_pos.reshape(pieces, width)

    def absorb_block(carried, item):
        block_rows, block_pos = item
        best, total, accum = carried
        scores = jnp.einsum(
            "cgrd,kgd->grck", grouped, block_rows[0], preferred_element_type=jnp.float32
        ) * head_dim ** (-0.5)
        key_line = block_pos[None, None, None, :]
        if summary:
            visible = key_line <= limits[:, :, :, None]
        else:
            visible = (
                (key_line > limits[:, :, :, None])
                & (key_line <= query_pos[None, None, :, None])
                & (key_line >= 0)
            )
        new_best = jnp.maximum(best, jnp.max(jnp.where(visible, scores, very_low), axis=-1))
        weights = jnp.where(visible, jnp.exp(scores - new_best[:, :, :, None]), 0.0)
        fade = jnp.exp(best - new_best)
        total = total * fade + jnp.sum(weights, axis=-1)
        accum = accum * fade[:, :, :, None] + jnp.einsum(
            "grck,kgd->grcd",
            weights.astype(jnp.bfloat16),
            block_rows[1],
            preferred_element_type=jnp.float32,
        )
        return ((new_best, total, accum), None)

    running, unused = lax.scan(absorb_block, running, (blocked, positions))
    return running


def body(queries, keys_values, band_widths, summary_blocks):
    rows = queries.shape[0]
    heads_kv = keys_values.shape[2] // HD
    heads_dev = band_widths.shape[0]
    ratio = heads_dev // heads_kv
    seq_index = lax.axis_index("seq")
    query_pos = seq_index * rows + jnp.arange(rows, dtype=jnp.int32)
    grouped = queries.reshape(rows, heads_kv, ratio, HD)
    limits = query_pos[None, None, :] - band_widths.reshape(heads_kv, ratio)[:, :, None]
    running = (
        jnp.full((heads_kv, ratio, rows), very_low, jnp.float32),
        jnp.zeros((heads_kv, ratio, rows), jnp.float32),
        jnp.zeros((heads_kv, ratio, rows, HD), jnp.float32),
    )
    reach = (BAND - 1) // rows + 1
    local_iota = jnp.arange(rows, dtype=jnp.int32)
    running = absorb(running, keys_values, query_pos, False, grouped, limits, query_pos)
    for distance in range(1, reach + 1):
        earlier = from_behind(keys_values, "seq", distance)
        running = absorb(
            running,
            earlier,
            (seq_index - distance) * rows + local_iota,
            False,
            grouped,
            limits,
            query_pos,
        )
    own_block = lax.dynamic_index_in_dim(summary_blocks, seq_index, 0, keepdims=False)
    local_block = own_block - seq_index * (rows // SB)
    summary_rows = lax.dynamic_slice_in_dim(keys_values, local_block * SB, SB, 1)
    summary_pos = (summary_blocks[:, None] * SB + jnp.arange(SB, dtype=jnp.int32)[None, :]).reshape(
        -1
    )
    gathered = lax.all_gather(summary_rows, "seq", axis=1, tiled=True)
    running = absorb(running, gathered, summary_pos, True, grouped, limits, query_pos)
    best, total, accum = running
    result = accum / total[:, :, :, None]
    return jnp.transpose(result, (2, 0, 1, 3)).reshape(rows, heads_dev * HD).astype(jnp.bfloat16)


def attend_kernel(
    rows, heads_kv, ratio, q_hbm, kv_hbm, widths, blocks, out_hbm,
    q_buf, kv_buf, vt_buf, acc_buf, best_buf, key_buf, own_keys, out_buf,
    q_sem, own_sem, out_sem, near_send, far_send, pass_send, recv_sem,
):
    me = lax.axis_index("seq")
    core = lax.rem(me, 2)
    partner = me + 1 - 2 * core
    seq_size = lax.axis_size("seq")
    heads = heads_kv * ratio
    scale = math.log2(math.e) * HD ** (-0.5)

    def remote(src, slot, g, send_sem, target):
        return pltpu.make_async_remote_copy(
            src_ref=src,
            dst_ref=kv_buf.at[slot, g],
            send_sem=send_sem,
            recv_sem=recv_sem.at[slot, g],
            device_id={"seq": target},
            device_id_type=pl.DeviceIdType.MESH,
        )

    def own_rows(g):
        return kv_hbm.at[:, :, g * HD : (g + 1) * HD]

    def own_copy(g):
        return pltpu.make_async_copy(own_rows(g), kv_buf.at[me, g], own_sem.at[g])

    def q_copy(h):
        return pltpu.make_async_copy(
            q_hbm.at[:, h * HD : (h + 1) * HD],
            q_buf.at[h // ratio, h % ratio],
            q_sem.at[h],
        )

    barrier = pltpu.get_barrier_semaphore()
    for step in range(1, seq_size):
        pl.semaphore_signal(
            barrier,
            inc=1,
            device_id={"seq": lax.rem(me + step, seq_size)},
            device_id_type=pl.DeviceIdType.MESH,
        )
    for g in range(heads_kv):
        own_copy(g).start()
    for h in range(heads):
        q_copy(h).start()
    pl.semaphore_wait(barrier, seq_size - 1)

    for g in range(heads_kv):
        own_copy(g).wait()

        @pl.when(me < 2)
        def _():
            remote(kv_buf.at[me, g], me, g, far_send.at[g], me + 2).start()

        @pl.when(core == 0)
        def _():
            remote(kv_buf.at[me, g], me, g, near_send.at[g], me + 1).start()

    for slot in range(seq_size):
        pos = slot * rows + lax.broadcasted_iota(jnp.int32, (rows, HD), 0)
        first = blocks[slot] * SB
        in_summary = (pos >= first) & (pos < first + SB)
        key_buf[slot] = jnp.where(in_summary, ALWAYS, pos)
    own_cols = lax.broadcasted_iota(jnp.int32, (rows, rows), 1)
    own_down = lax.broadcasted_iota(jnp.int32, (rows, rows), 0)
    own_line = jnp.concatenate([key_buf[me]] * (rows // HD), axis=1)
    own_keys[...] = jnp.where(own_down <= own_cols, own_line, -ALWAYS)
    for g in range(heads_kv):
        vt_buf[g, HD:, :] = jnp.ones((ONES, rows), jnp.bfloat16)

    row_pos = me * rows + lax.broadcasted_iota(jnp.int32, (1, rows), 1)

    def heads_of(slot, g, is_own):
        vt_buf[g, :HD, :] = kv_buf[slot, g, 1].astype(jnp.float32).T.astype(jnp.bfloat16)

        def score(r):
            return lax.dot_general(
                kv_buf[slot, g, 0],
                q_buf[g, r],
                (((1,), (1,)), ((), ())),
                preferred_element_type=jnp.float32,
            )

        def soften(r, scores):
            limit = row_pos - widths[g * ratio + r]
            if is_own:
                keys = own_keys[...]
            else:
                keys = jnp.concatenate([key_buf[slot]] * (rows // HD), axis=1)
            scores = jnp.where(keys > limit, scores, -1e30)
            top = jnp.max(scores, axis=0, keepdims=True)
            fade = None
            if not is_own:
                old = best_buf[g, r]
                top = jnp.maximum(old, top)
                fade = jnp.exp2((old - top) * scale)
            best_buf[g, r] = top
            return jnp.exp2((scores - top) * scale).astype(jnp.bfloat16), fade

        def mix(r, weights, fade):
            part = lax.dot_general(
                vt_buf[g],
                weights,
                (((1,), (0,)), ((), ())),
                preferred_element_type=jnp.float32,
            )[: HD + STAT]
            if fade is not None:
                part = part + acc_buf[g, r] * fade
            acc_buf[g, r] = part

        scores = score(0)
        waiting = None
        for r in range(ratio):
            following = score(r + 1) if r + 1 < ratio else None
            if waiting is not None:
                mix(*waiting)
            waiting = (r, *soften(r, scores))
            scores = following
        mix(*waiting)

    for h in range(heads):
        q_copy(h).wait()

    def own_step(g, unused):
        heads_of(me, g, True)
        return unused

    lax.fori_loop(0, heads_kv, own_step, 0)

    def out_copy(h):
        return pltpu.make_async_copy(
            out_buf.at[h],
            out_hbm.at[:, pl.ds(pl.multiple_of(h * HD, HD), HD)],
            out_sem.at[h],
        )

    def finish(g):
        for r in range(ratio):
            total = acc_buf[g, r, HD : HD + 1, :]
            result = acc_buf[g, r, :HD, :] * (1.0 / total)
            out_buf[g * ratio + r] = result.T.astype(out_buf.dtype)
            if r % 2:
                out_copy(g * ratio + r - 1).start()
                out_copy(g * ratio + r).start()

    near = heads_kv * core

    def other_step(item, unused):
        far = item - near
        is_near = item < near
        far_slot = jnp.where(lax.rem(far, 2) == 0, core, 1 - core)
        slot = jnp.where(is_near, me - 1, far_slot)
        g = jnp.where(is_near, item, far // 2)
        remote(kv_buf.at[slot, g], slot, g, pass_send.at[g], partner).wait_recv()

        @pl.when((me >= 2) & (slot == core))
        def _():
            remote(kv_buf.at[slot, g], slot, g, pass_send.at[g], partner).start()

        heads_of(slot, g, False)

        @pl.when((me >= 2) & (item >= near) & (lax.rem(far, 2) == 1))
        def _():
            finish(g)

        return unused

    lax.fori_loop(0, heads_kv * me, other_step, 0)

    def last_step(g, unused):
        finish(g)
        return unused

    lax.fori_loop(0, jnp.where(me < 2, heads_kv, 0), last_step, 0)

    for g in range(heads_kv):

        @pl.when(me < 2)
        def _():
            remote(kv_buf.at[me, g], me, g, far_send.at[g], me + 2).wait_send()

        @pl.when(core == 0)
        def _():
            remote(kv_buf.at[me, g], me, g, near_send.at[g], me + 1).wait_send()

        @pl.when(me >= 2)
        def _():
            remote(kv_buf.at[core, g], core, g, pass_send.at[g], partner).wait_send()

    for h in range(heads):
        out_copy(h).wait()


def move_kernel(pieces, src_hbm, dst_hbm, held, in_sem, out_sem):
    rows = held.shape[1]

    def fetch(i):
        return pltpu.make_async_copy(
            src_hbm.at[i * rows : (i + 1) * rows], held.at[i], in_sem.at[i]
        )

    def store(i):
        return pltpu.make_async_copy(
            held.at[i], dst_hbm.at[i * rows : (i + 1) * rows], out_sem.at[i]
        )

    for i in range(pieces):
        fetch(i).start()
    for i in range(pieces):
        fetch(i).wait()
        store(i).start()
    for i in range(pieces):
        store(i).wait()


def move(result):
    rows, columns = result.shape
    pieces = 8
    outside = pl.BlockSpec(memory_space=pltpu.HBM)
    return pl.pallas_call(
        functools.partial(move_kernel, pieces),
        out_shape=jax.ShapeDtypeStruct(result.shape, result.dtype),
        in_specs=[outside],
        out_specs=outside,
        scratch_shapes=[
            pltpu.VMEM((pieces, rows // pieces, columns), result.dtype),
            pltpu.SemaphoreType.DMA((pieces,)),
            pltpu.SemaphoreType.DMA((pieces,)),
        ],
        compiler_params=pltpu.CompilerParams(vmem_limit_bytes=63 * 1024 * 1024),
    )(result)


def fused_body(queries, keys_values, band_widths, summary_blocks):
    rows = queries.shape[0]
    heads_kv = keys_values.shape[2] // HD
    heads = band_widths.shape[0]
    ratio = heads // heads_kv
    seq_size = lax.axis_size("seq")
    outside = pl.BlockSpec(memory_space=pltpu.HBM)
    scalars = pl.BlockSpec(memory_space=pltpu.SMEM)
    dma = pltpu.SemaphoreType.DMA
    attended = pl.pallas_call(
        functools.partial(attend_kernel, rows, heads_kv, ratio),
        out_shape=jax.ShapeDtypeStruct(queries.shape, jnp.bfloat16),
        in_specs=[outside, outside, scalars, scalars],
        out_specs=outside,
        scratch_shapes=[
            pltpu.VMEM((heads_kv, ratio, rows, HD), jnp.bfloat16),
            pltpu.VMEM((seq_size, heads_kv, 2, rows, HD), jnp.bfloat16),
            pltpu.VMEM((heads_kv, HD + ONES, rows), jnp.bfloat16),
            pltpu.VMEM((heads_kv, ratio, HD + STAT, rows), jnp.float32),
            pltpu.VMEM((heads_kv, ratio, 1, rows), jnp.float32),
            pltpu.VMEM((seq_size, rows, HD), jnp.int32),
            pltpu.VMEM((rows, rows), jnp.int32),
            pltpu.VMEM((heads, rows, HD), jnp.bfloat16),
            dma((heads,)),
            dma((heads_kv,)),
            dma((heads,)),
            dma((heads_kv,)),
            dma((heads_kv,)),
            dma((heads_kv,)),
            dma((seq_size, heads_kv)),
        ],
        compiler_params=pltpu.CompilerParams(
            collective_id=0,
            has_side_effects=True,
            vmem_limit_bytes=63 * 1024 * 1024,
        ),
        cost_estimate=pl.CostEstimate(
            flops=4 * heads * rows * rows * seq_size * HD,
            bytes_accessed=4 * queries.size,
            transcendentals=heads * rows * rows * seq_size,
        ),
    )(queries, keys_values, band_widths, summary_blocks)
    return move(attended)


def dispatch(queries, keys_values, band_widths, summary_blocks):
    rows = queries.shape[0]
    seq_size = lax.axis_size("seq")
    two_chips = seq_size == 4 and summary_blocks.shape[0] == seq_size
    if two_chips and seq_size * rows <= BAND and rows % (2 * SB) == 0:
        return fused_body(queries, keys_values, band_widths, summary_blocks)
    return body(queries, keys_values, band_widths, summary_blocks)


def solution(mesh):
    return jax.shard_map(
        dispatch,
        mesh=mesh,
        in_specs=(
            P(("grp", "seq"), "kvh"),
            P(None, ("grp", "seq"), "kvh"),
            P(("grp", "kvh")),
            P("grp"),
        ),
        out_specs=P(("grp", "seq"), "kvh"),
        check_vma=False,
    )
```
